32 devices in a mesh: ctx: 8 (over z, x), head: 4 (over y, core).
Axes of the slice: x: 2, y: 2, z: 4, core: 2. Of those that a mesh axis runs over, the one named last changes fastest.
Arguments:
- query_in: bfloat16 [4096, 2048], P('ctx', 'head'), may hold values from -6 to 6
- key_in: bfloat16 [4096, 2048], P('ctx', 'head'), may hold values from -6 to 6
- value_in: bfloat16 [4096, 4096], P('ctx', 'head'), may hold values from -6 to 6
- query_taps: float32 [4, 2048], P(None, 'head'), may hold values from -3 to 3
- key_taps: float32 [4, 2048], P(None, 'head'), may hold values from -3 to 3
- value_taps: float32 [4, 4096], P(None, 'head'), may hold values from -3 to 3
- log_decay: float32 [32, 4096], P('head', 'ctx'), may hold values from -2 to 0
- beta_logit: float32 [32, 4096], P('head', 'ctx'), may hold values from -9 to 2
- gate_in: bfloat16 [4096, 4096], P('ctx', 'head'), may hold values from -6 to 6
- norm_gain: float32 [128], replicated, may hold values from 0.1 to 1.9
Outputs:
- core_out: bfloat16 [4096, 4096], P(('ctx', 'head'))
The draws below stay inside these ranges and needn't reach their ends.
All inputs are finite; a program needn't handle non-finite values.
Results may differ from the reference program's by a relative error of at most 0.005.
Values may be sent and summed in bfloat16 or wider, within the bound.
A program may use at most 64 MiB of HBM per device.

```python
import jax
import jax.numpy as jnp
from jax import lax

DK = 128
KH = 16
OUTPUT_CHANNELS = 32
CONV = 4
GROUP = 64
TOK_DEV = 512
INPUT_LENGTH = 4096


def head_kinds(key):
    share = 0.5
    return jax.random.bernoulli(jax.random.fold_in(key, 11), share, (OUTPUT_CHANNELS,))


def draw_log_decay(key, part):
    lagging_channels = head_kinds(key)
    block_count = INPUT_LENGTH // TOK_DEV
    block_factor = jnp.exp(jax.random.uniform(jax.random.fold_in(key, 21), (OUTPUT_CHANNELS, block_count), jnp.float32, -0.7, 0.7))
    factor = jnp.repeat(block_factor, TOK_DEV, axis=1)
    rough = jnp.exp(jax.random.uniform(jax.random.fold_in(key, 22), (OUTPUT_CHANNELS, INPUT_LENGTH), jnp.float32, -0.7, 0.7))
    fast_rate = rough * factor / 40.0
    slow_rate = rough * factor * 0.8 / INPUT_LENGTH
    forgetting_speed = jnp.where(lagging_channels[:, None], slow_rate, fast_rate)
    sequence_indices = jax.random.randint(jax.random.fold_in(key, 23), (OUTPUT_CHANNELS, 3), 0, INPUT_LENGTH)
    kept_fraction = jax.random.uniform(jax.random.fold_in(key, 24), (OUTPUT_CHANNELS, 3), jnp.float32, 0.6, 0.8)
    lines_by_channel = jnp.broadcast_to(jnp.arange(OUTPUT_CHANNELS)[:, None], (OUTPUT_CHANNELS, 3))
    spike_clusters = jnp.zeros((OUTPUT_CHANNELS, INPUT_LENGTH), jnp.float32).at[lines_by_channel, sequence_indices].add(jnp.log(kept_fraction))
    spike_clusters = jnp.where(lagging_channels[:, None], spike_clusters, 0.0)
    return (spike_clusters - forgetting_speed).astype(jnp.float32)


def draw_beta_logit(key, part):
    lagging_channels = head_kinds(key)
    rough = jnp.exp(jax.random.uniform(jax.random.fold_in(key, 31), (OUTPUT_CHANNELS, INPUT_LENGTH), jnp.float32, -0.7, 0.7))
    fast_logit = jnp.clip(jax.random.normal(jax.random.fold_in(key, 32), (OUTPUT_CHANNELS, INPUT_LENGTH), jnp.float32), -2.0, 2.0)
    small = jnp.minimum(38.0 / INPUT_LENGTH * rough, 0.5)
    slow_logit = jnp.log(small) - jnp.log1p(-small)
    return jnp.where(lagging_channels[:, None], slow_logit, fast_logit).astype(jnp.float32)


def level_of(stream_key, shape, cuts, low, high):
    level = 1.0
    for dim, shards_of in cuts:
        steps = jax.random.uniform(jax.random.fold_in(jax.random.fold_in(stream_key, 6), dim), (shards_of,), jnp.float32, low / len(cuts), high / len(cuts))
        level = level * jnp.repeat(jnp.exp(steps), shape[dim] // shards_of).reshape((-1,) + (1,) * (len(shape) - 1 - dim))
    return level


def bell_draw(stream_key, dims, deviation, reach, pieces=(), kind=jnp.bfloat16):
    entries = deviation * jax.random.normal(stream_key, dims, jnp.float32)
    if pieces:
        entries = entries * level_of(stream_key, dims, pieces, -0.22, 0.18)
    return jnp.clip(entries, -reach, reach).astype(kind)


def setup_inputs(seed: int = 0) -> dict:
    key_of = jax.random.split(jax.random.key(seed), 11)
    query_in = bell_draw(key_of[0], (INPUT_LENGTH, KH * DK), 1.0, 6.0, ((0, 8), (1, 4)))
    key_in = bell_draw(key_of[1], (INPUT_LENGTH, KH * DK), 1.0, 6.0, ((0, 8), (1, 4)))
    value_in = bell_draw(key_of[2], (INPUT_LENGTH, OUTPUT_CHANNELS * DK), 1.0, 6.0, ((0, 8), (1, 4)))
    query_taps = bell_draw(key_of[3], (CONV, KH * DK), CONV ** -0.5, 3.0, ((1, 4),), jnp.float32)
    key_taps = bell_draw(key_of[4], (CONV, KH * DK), CONV ** -0.5, 3.0, ((1, 4),), jnp.float32)
    value_taps = bell_draw(key_of[5], (CONV, OUTPUT_CHANNELS * DK), CONV ** -0.5, 3.0, ((1, 4),), jnp.float32)
    log_decay = draw_log_decay(jax.random.fold_in(key_of[10], 71), 0)
    beta_logit = draw_beta_logit(jax.random.fold_in(key_of[10], 71), 0)
    gate_in = bell_draw(key_of[8], (INPUT_LENGTH, OUTPUT_CHANNELS * DK), 1.0, 6.0, ((0, 8), (1, 4)))
    norm_gain = jnp.clip(1.0 + 0.18 * jax.random.normal(key_of[9], (DK,), jnp.float32), 0.1, 1.9)
    return {"query_in": query_in, "key_in": key_in, "value_in": value_in, "query_taps": query_taps, "key_taps": key_taps, "value_taps": value_taps, "log_decay": log_decay, "beta_logit": beta_logit, "gate_in": gate_in, "norm_gain": norm_gain}


highest = lax.Precision.HIGHEST
norm_eps = 1e-06

def causal_conv(joined, taps, length):
    weights = taps.astype(jnp.float32)
    summed = jnp.zeros((length, joined.shape[1]), jnp.float32)
    for offset in range(weights.shape[0]):
        summed = summed + weights[offset] * joined[offset:offset + length].astype(jnp.float32)
    return jax.nn.silu(summed)

def unit_rows(matrix):
    return matrix * lax.rsqrt(lax.optimization_barrier(jnp.sum(matrix * matrix, axis=-1, keepdims=True)) + norm_eps)

def group_terms(query, keys, values, beta, logdecay):
    length = logdecay.shape[-1]
    cumul = jnp.cumsum(logdecay, axis=-1)
    row_ids = lax.broadcasted_iota(jnp.int32, (length, length), 0)
    col_ids = lax.broadcasted_iota(jnp.int32, (length, length), 1)
    inside = col_ids <= row_ids
    differ = cumul[..., :, None] - cumul[..., None, :]
    decay_mask = jnp.where(inside, jnp.exp(jnp.where(inside, differ, 0.0)), 0.0)
    keygram = jnp.einsum('...ik,...jk->...ij', keys, keys, precision=highest)
    strict = jnp.where(col_ids < row_ids, beta[..., :, None] * keygram * decay_mask, 0.0)
    identity_mats = jnp.broadcast_to(jnp.eye(length, dtype=jnp.float32), strict.shape)
    inverse = lax.linalg.triangular_solve(identity_mats + strict, identity_mats, left_side=True, lower=True, unit_diagonal=True)
    upd_values = jnp.einsum('...ij,...jd->...id', inverse, beta[..., None] * values, precision=highest)
    upd_keys = jnp.einsum('...ij,...jd->...id', inverse, (beta * jnp.exp(cumul))[..., None] * keys, precision=highest)
    scores = jnp.einsum('...ik,...jk->...ij', query, keys, precision=highest) * decay_mask
    last_log = cumul[..., -1:]
    query_decay = query * jnp.exp(cumul)[..., None]
    key_decay = keys * jnp.exp(last_log - cumul)[..., None]
    return (upd_values, upd_keys, scores, query_decay, key_decay, last_log[..., 0])

def group_step(state, terms):
    upd_values, upd_keys, scores, query_decay, key_decay, last_log = terms
    new_values = upd_values - jnp.einsum('...ik,...kd->...id', upd_keys, state, precision=highest)
    output = jnp.einsum('...ik,...kd->...id', query_decay, state, precision=highest)
    output = output + jnp.einsum('...ij,...jd->...id', scores, new_values, precision=highest)
    state = jnp.exp(last_log)[..., None, None] * state + jnp.einsum('...ik,...id->...kd', key_decay, new_values, precision=highest)
    return (state, output)

def reference(query_in, key_in, value_in, query_taps, key_taps, value_taps, log_decay, beta_logit, gate_in, norm_gain):
    tokens_all = query_in.shape[0]
    rim_width = CONV - 1

    def padded(inputs):
        return jnp.concatenate([jnp.zeros((rim_width, inputs.shape[1]), jnp.bfloat16), inputs], axis=0)
    query_conv = causal_conv(padded(query_in), query_taps, tokens_all)
    key_conv = causal_conv(padded(key_in), key_taps, tokens_all)
    value_conv = causal_conv(padded(value_in), value_taps, tokens_all)
    queries = (unit_rows(query_conv.reshape(tokens_all, KH, DK)) * DK ** (-0.5)).astype(jnp.bfloat16)
    keys = unit_rows(key_conv.reshape(tokens_all, KH, DK)).astype(jnp.bfloat16)
    values = value_conv.reshape(tokens_all, OUTPUT_CHANNELS, DK).astype(jnp.bfloat16)
    beta = jax.nn.sigmoid(beta_logit)
    gates = gate_in.reshape(tokens_all, OUTPUT_CHANNELS, DK)
    groups_all = tokens_all // GROUP

    def per_head(head_index):
        key_index = head_index // (OUTPUT_CHANNELS // KH)
        query_head = lax.dynamic_index_in_dim(queries, key_index, 1, keepdims=False).astype(jnp.float32).reshape(groups_all, GROUP, DK)
        key_head = lax.dynamic_index_in_dim(keys, key_index, 1, keepdims=False).astype(jnp.float32).reshape(groups_all, GROUP, DK)
        value_head = lax.dynamic_index_in_dim(values, head_index, 1, keepdims=False).astype(jnp.float32).reshape(groups_all, GROUP, DK)
        beta_head = lax.dynamic_index_in_dim(beta, head_index, 0, keepdims=False).reshape(groups_all, GROUP)
        decay_head = lax.dynamic_index_in_dim(log_decay, head_index, 0, keepdims=False).reshape(groups_all, GROUP)
        terms = group_terms(query_head, key_head, value_head, beta_head, decay_head)
        _, outputs = lax.scan(group_step, jnp.zeros((DK, DK), jnp.float32), terms)
        output = outputs.reshape(tokens_all, DK)
        gate = lax.dynamic_index_in_dim(gates, head_index, 1, keepdims=False).astype(jnp.float32)
        normed = output * lax.rsqrt(lax.optimization_barrier(jnp.mean(output * output, axis=-1, keepdims=True)) + norm_eps) * norm_gain * jax.nn.silu(gate)
        return normed.astype(jnp.bfloat16)
    stacked = lax.map(per_head, jnp.arange(OUTPUT_CHANNELS, dtype=jnp.int32))
    return stacked.transpose(1, 0, 2).reshape(tokens_all, OUTPUT_CHANNELS * DK)
```

```python
import functools

import jax
import jax.numpy as jnp
from jax import lax
from jax.experimental import pallas as pl
from jax.experimental.pallas import tpu as pltpu
from jax.sharding import PartitionSpec as P

CHUNK = 128
PAD = 16
norm_eps = 1e-06
bf16 = jnp.bfloat16
f32 = jnp.float32
highest = lax.Precision.HIGHEST


def split(x):
    hi = x.astype(bf16)
    return hi, (x - hi.astype(f32)).astype(bf16)


def dot1(a, b):
    return jnp.dot(a, b, preferred_element_type=f32)


def dot3(a, b):
    (ah, al), (bh, bl) = a, b
    return dot1(jnp.concatenate([ah, al], axis=1), jnp.concatenate([bh, bh], axis=0)) + dot1(ah, bl)


def silu(x):
    return x / (1.0 + jnp.exp(-x))


def conv(buf, tail_ref, in_ref, taps_ref):
    length = in_ref.shape[0]
    count = taps_ref.shape[0]
    buf[0:PAD, :] = tail_ref[...].astype(f32)
    buf[PAD:, :] = in_ref[...].astype(f32)
    total = None
    for j in range(count):
        term = taps_ref[j : j + 1, :] * buf[pl.ds(PAD - count + 1 + j, length), :]
        total = term if total is None else total + term
    return silu(total)


def unit(x):
    return x * lax.rsqrt(jnp.sum(x * x, axis=-1, keepdims=True) + norm_eps)


def local_kernel(
    q_ref, k_ref, v_ref, qt_ref, kt_ref, vt_ref, qw_ref, kw_ref, vw_ref, ld_ref, bl_ref,
    out_ref, eff_ref, state_ref, prod_ref, qbuf, vbuf,
):
    length, dim = q_ref.shape
    ratio = v_ref.shape[1] // dim
    q_all = (unit(conv(qbuf, qt_ref, q_ref, qw_ref)) * dim ** (-0.5)).astype(bf16)
    k_all = unit(conv(qbuf, kt_ref, k_ref, kw_ref)).astype(bf16)
    v_all = conv(vbuf, vt_ref, v_ref, vw_ref).astype(bf16)

    size = CHUNK
    rows = lax.broadcasted_iota(jnp.int32, (size, size), 0)
    cols = lax.broadcasted_iota(jnp.int32, (size, size), 1)
    inside = cols <= rows
    strictly = cols < rows
    eye = jnp.where(cols == rows, 1.0, 0.0).astype(f32)
    upper = jnp.where(rows <= cols, 1.0, 0.0).astype(f32)
    masks = []
    width = 1
    while width < size:
        pick = (rows // (2 * width) == cols // (2 * width)) & (rows // width != cols // width)
        masks.append(jnp.where(pick & strictly, 1.0, 0.0).astype(bf16))
        width *= 2

    beta_all = 1.0 / (1.0 + jnp.exp(-bl_ref[0]))
    items = []
    for c in range(length // size):
        span = slice(c * size, (c + 1) * size)
        kc, qc = k_all[span], q_all[span]
        kf, qf = kc.astype(f32), qc.astype(f32)
        k_turn = kf.T
        nt = (((1,), (1,)), ((), ()))
        gram = lax.dot_general(kc, kc, nt, preferred_element_type=f32)
        qk = lax.dot_general(qc, kc, nt, preferred_element_type=f32)
        cum = lax.dot_general(
            ld_ref[0][:, span], upper, (((1,), (0,)), ((), ())),
            precision=highest, preferred_element_type=f32,
        )
        stacked = jnp.concatenate(
            [cum, beta_all[:, span], jnp.zeros((8 - 2 * ratio, size), f32)], axis=0
        )
        turned = stacked.T
        for h in range(ratio):
            cum_row = cum[h : h + 1]
            cum_col = turned[:, h : h + 1]
            beta_col = turned[:, ratio + h : ratio + h + 1]
            last = cum_row[:, size - 1 :]
            mask = jnp.where(inside, jnp.exp(jnp.where(inside, cum_col - cum_row, 0.0)), 0.0)
            low = split(jnp.where(strictly, beta_col * gram * mask, 0.0))
            grow = jnp.exp(cum_col)
            vf = v_all[span, h * dim : (h + 1) * dim].astype(f32)
            items.append(dict(
                c=c, h=h, low=low,
                x=eye - (low[0] * masks[0]).astype(f32) - (low[1] * masks[0]).astype(f32),
                rhs=split(jnp.concatenate([beta_col * vf, (beta_col * grow) * kf], axis=1)),
                scores=(qk * mask),
                qd=qf * grow,
                kd=k_turn * jnp.exp(last - cum_row),
                keep=jnp.exp(last),
            ))
    for mask in masks[1:]:
        for it in items:
            x = split(it["x"])
            part = dot3(x, (it["low"][0] * mask, it["low"][1] * mask))
            it["x"] = it["x"] - dot3(split(part), x)
    for it in items:
        it["uw"] = dot3(split(it["x"]), it["rhs"])
    states = [None] * ratio
    for it in items:
        c, h = it["c"], it["h"]
        u, w = it["uw"][:, :dim], it["uw"][:, dim:]
        zero = jnp.zeros((size, dim), f32)
        if c == 0:
            new = jnp.concatenate([u, -w], axis=1)
            seen = jnp.concatenate([zero, it["qd"]], axis=1)
            kept = jnp.concatenate([jnp.zeros((dim, dim), f32), it["keep"] * eye], axis=1)
        else:
            both = split(jnp.concatenate([w, it["qd"]], axis=0))
            got = dot3(both, split(states[h]))
            new = jnp.concatenate([u, zero], axis=1) - got[:size]
            seen = got[size:]
            kept = it["keep"] * states[h]
        new = split(new)
        out = seen + dot3(split(it["scores"]), new)
        states[h] = kept + dot3(split(it["kd"]), new)
        span = pl.ds(c * size, size)
        out_ref[span, h * dim : (h + 1) * dim] = out[:, :dim]
        eff_ref[span, h * dim : (h + 1) * dim] = out[:, dim:]
    for h in range(ratio):
        state_ref[h] = states[h][:, :dim]
        prod_ref[h] = states[h][:, dim:]


def final_kernel(out_ref, eff_ref, inc_ref, gate_ref, gain_ref, res_ref):
    core = out_ref[...] + dot3(split(eff_ref[...]), split(inc_ref[0]))
    gate = gate_ref[...].astype(f32)
    normed = core * lax.rsqrt(jnp.mean(core * core, axis=-1, keepdims=True) + norm_eps)
    res_ref[...] = (normed * gain_ref[...] * silu(gate)).astype(bf16)


def shifted(value, axis, steps):
    count = lax.axis_size(axis)
    first, last = (max(0, -steps), min(count, count - steps))
    return lax.ppermute(value, axis, [(source, source + steps) for source in range(first, last)])


def body(
    query_in, key_in, value_in, query_taps, key_taps, value_taps,
    log_decay, beta_logit, gate_in, norm_gain,
):
    dim = norm_gain.shape[0]
    length = query_in.shape[0]
    value_heads = log_decay.shape[0]
    key_heads = query_in.shape[1] // dim
    ratio = value_heads // key_heads
    taps = query_taps.shape[0]
    tails = shifted(
        jnp.concatenate([query_in[-PAD:], key_in[-PAD:], value_in[-PAD:]], axis=1), "ctx", 1
    )
    wide = ratio * dim

    def block(rows, width, first=0):
        return pl.BlockSpec((rows, width), lambda i: (0, first + i))

    rates = pl.BlockSpec((1, ratio, length), lambda i: (i, 0, 0))
    mats = pl.BlockSpec((ratio, dim, dim), lambda i: (i, 0, 0))
    mat_shape = jax.ShapeDtypeStruct((value_heads, dim, dim), f32)
    wide_shape = jax.ShapeDtypeStruct((length, value_heads * dim), f32)
    local_out, effect, local_state, product = pl.pallas_call(
        local_kernel,
        grid=(key_heads,),
        in_specs=[
            block(length, dim), block(length, dim), block(length, wide),
            block(PAD, dim), block(PAD, dim, key_heads), block(PAD, wide, 2 * key_heads // ratio),
            block(taps, dim), block(taps, dim), block(taps, wide),
            rates, rates,
        ],
        out_specs=[block(length, wide), block(length, wide), mats, mats],
        out_shape=[wide_shape, wide_shape, mat_shape, mat_shape],
        scratch_shapes=[
            pltpu.VMEM((length + PAD, dim), f32),
            pltpu.VMEM((length + PAD, wide), f32),
        ],
        compiler_params=pltpu.CompilerParams(vmem_limit_bytes=48 * 1024 * 1024),
        name="local",
    )(
        query_in, key_in, value_in, tails, tails, tails, query_taps, key_taps, value_taps,
        log_decay.reshape(key_heads, ratio, length), beta_logit.reshape(key_heads, ratio, length),
    )

    def chain_turn(turn, incoming):
        moved = jnp.einsum("hij,hjk->hik", product, incoming, precision=highest)
        return shifted(moved + local_state, "ctx", 1)

    zero_state = jnp.zeros((value_heads, dim, dim), f32)
    incoming = lax.fori_loop(0, lax.axis_size("ctx") - 1, chain_turn, zero_state)

    normed = pl.pallas_call(
        final_kernel,
        grid=(value_heads,),
        in_specs=[
            block(length, dim), block(length, dim),
            pl.BlockSpec((1, dim, dim), lambda i: (i, 0, 0)),
            block(length, dim),
            pl.BlockSpec((1, dim), lambda i: (0, 0)),
        ],
        out_specs=block(length, dim),
        out_shape=jax.ShapeDtypeStruct((length, value_heads * dim), bf16),
        compiler_params=pltpu.CompilerParams(vmem_limit_bytes=48 * 1024 * 1024),
        name="final",
    )(local_out, effect, incoming, gate_in, norm_gain.reshape(1, dim))
    return lax.all_to_all(normed, "head", split_axis=0, concat_axis=1, tiled=True)


def solution(mesh):
    in_specs = (
        P("ctx", "head"), P("ctx", "head"), P("ctx", "head"),
        P(None, "head"), P(None, "head"), P(None, "head"),
        P("head", "ctx"), P("head", "ctx"), P("ctx", "head"), P(),
    )
    out_specs = P(("ctx", "head"), None)
    return jax.shard_map(body, mesh=mesh, in_specs=in_specs, out_specs=out_specs, check_vma=False)
```

```python
import functools

import jax
import jax.numpy as jnp
from jax import lax
from jax.experimental import pallas as pl
from jax.experimental.pallas import tpu as pltpu
from jax.sharding import PartitionSpec as P

CHUNK = 128
PAD = 16
norm_eps = 1e-06
bf16 = jnp.bfloat16
f32 = jnp.float32
highest = lax.Precision.HIGHEST


def split(x):
    hi = x.astype(bf16)
    return hi, (x - hi.astype(f32)).astype(bf16)


def dot1(a, b):
    return jnp.dot(a, b, preferred_element_type=f32)


def dot3(a, b):
    (ah, al), (bh, bl) = a, b
    return dot1(jnp.concatenate([ah, al], axis=1), jnp.concatenate([bh, bh], axis=0)) + dot1(ah, bl)


def silu(x):
    return x / (1.0 + jnp.exp(-x))


def conv(buf, tail_ref, in_ref, taps_ref):
    length = in_ref.shape[0]
    count = taps_ref.shape[0]
    buf[0:PAD, :] = tail_ref[...].astype(f32)
    buf[PAD:, :] = in_ref[...].astype(f32)
    total = None
    for j in range(count):
        term = taps_ref[j : j + 1, :] * buf[pl.ds(PAD - count + 1 + j, length), :]
        total = term if total is None else total + term
    return silu(total)


def unit(x):
    return x * lax.rsqrt(jnp.sum(x * x, axis=-1, keepdims=True) + norm_eps)


def local_kernel(
    q_ref, k_ref, v_ref, qt_ref, kt_ref, vt_ref, qw_ref, kw_ref, vw_ref, ld_ref, bl_ref,
    out_ref, eff_ref, state_ref, prod_ref, qbuf, vbuf,
):
    length, dim = q_ref.shape
    ratio = v_ref.shape[1] // dim
    q_all = (unit(conv(qbuf, qt_ref, q_ref, qw_ref)) * dim ** (-0.5)).astype(bf16)
    k_all = unit(conv(qbuf, kt_ref, k_ref, kw_ref)).astype(bf16)
    v_all = conv(vbuf, vt_ref, v_ref, vw_ref).astype(bf16)

    size = CHUNK
    rows = lax.broadcasted_iota(jnp.int32, (size, size), 0)
    cols = lax.broadcasted_iota(jnp.int32, (size, size), 1)
    inside = cols <= rows
    strictly = cols < rows
    eye = jnp.where(cols == rows, 1.0, 0.0).astype(f32)
    upper = jnp.where(rows <= cols, 1.0, 0.0).astype(f32)
    masks = []
    width = 1
    while width < size:
        pick = (rows // (2 * width) == cols // (2 * width)) & (rows // width != cols // width)
        masks.append(jnp.where(pick & strictly, 1.0, 0.0).astype(bf16))
        width *= 2

    beta_all = 1.0 / (1.0 + jnp.exp(-bl_ref[0]))
    items = []
    for c in range(length // size):
        span = slice(c * size, (c + 1) * size)
        kc, qc = k_all[span], q_all[span]
        kf, qf = kc.astype(f32), qc.astype(f32)
        k_turn = kf.T
        nt = (((1,), (1,)), ((), ()))
        gram = lax.dot_general(kc, kc, nt, preferred_element_type=f32)
        qk = lax.dot_general(qc, kc, nt, preferred_element_type=f32)
        cum = lax.dot_general(
            ld_ref[0][:, span], upper, (((1,), (0,)), ((), ())),
            precision=highest, preferred_element_type=f32,
        )
        stacked = jnp.concatenate(
            [cum, beta_all[:, span], jnp.zeros((8 - 2 * ratio, size), f32)], axis=0
        )
        turned = stacked.T
        for h in range(ratio):
            cum_row = cum[h : h + 1]
            cum_col = turned[:, h : h + 1]
            beta_col = turned[:, ratio + h : ratio + h + 1]
            last = cum_row[:, size - 1 :]
            mask = jnp.where(inside, jnp.exp(jnp.where(inside, cum_col - cum_row, 0.0)), 0.0)
            low = split(jnp.where(strictly, beta_col * gram * mask, 0.0))
            grow = jnp.exp(cum_col)
            vf = v_all[span, h * dim : (h + 1) * dim].astype(f32)
            items.append(dict(
                c=c, h=h, low=low,
                x=eye - (low[0] * masks[0]).astype(f32) - (low[1] * masks[0]).astype(f32),
                rhs=split(jnp.concatenate([beta_col * vf, (beta_col * grow) * kf], axis=1)),
                scores=(qk * mask),
                qd=qf * grow,
                kd=k_turn * jnp.exp(last - cum_row),
                keep=jnp.exp(last),
            ))
    for mask in masks[1:]:
        for it in items:
            x = it["x"].astype(bf16)
            part = dot1(x, it["low"][0] * mask)
            it["x"] = it["x"] - dot1(part.astype(bf16), x)
    for it in items:
        x = split(it["x"])
        rest = (eye - it["x"]) - dot3(it["low"], x)
        it["x"] = it["x"] + dot1(x[0], rest.astype(bf16))
    for it in items:
        it["uw"] = dot3(split(it["x"]), it["rhs"])
    states = [None] * ratio
    for it in items:
        c, h = it["c"], it["h"]
        u, w = it["uw"][:, :dim], it["uw"][:, dim:]
        zero = jnp.zeros((size, dim), f32)
        if c == 0:
            new = jnp.concatenate([u, -w], axis=1)
            seen = jnp.concatenate([zero, it["qd"]], axis=1)
            kept = jnp.concatenate([jnp.zeros((dim, dim), f32), it["keep"] * eye], axis=1)
        else:
            both = split(jnp.concatenate([w, it["qd"]], axis=0))
            got = dot3(both, split(states[h]))
            new = jnp.concatenate([u, zero], axis=1) - got[:size]
            seen = got[size:]
            kept = it["keep"] * states[h]
        new = split(new)
        out = seen + dot1(it["scores"].astype(bf16), new[0])
        states[h] = kept + dot3(split(it["kd"]), new)
        span = pl.ds(c * size, size)
        out_ref[span, h * dim : (h + 1) * dim] = out[:, :dim]
        eff_ref[span, h * dim : (h + 1) * dim] = out[:, dim:]
    for h in range(ratio):
        state_ref[h] = states[h][:, :dim]
        prod_ref[h] = states[h][:, dim:]


def carry_kernel(
    ring, peers, out_ref, eff_ref, state_ref, prod_ref, gate_ref, gain_ref, res_ref,
    incoming, outgoing, stage, ring_send, ring_recv, peer_send, peer_recv,
):
    heads, dim, _ = state_ref.shape
    rows = res_ref.shape[0]
    me = lax.axis_index("ctx")
    mine = lax.axis_index("head")
    after, before = lax.rem(me + 1, ring), lax.rem(me + ring - 1, ring)
    partners = [lax.rem(mine + d, peers) for d in range(1, peers)]
    barrier = pltpu.get_barrier_semaphore()
    for other in (after, before):
        pl.semaphore_signal(
            barrier, inc=1, device_id=(other, mine), device_id_type=pl.DeviceIdType.MESH
        )
    for other in partners:
        pl.semaphore_signal(
            barrier, inc=1, device_id=(me, other), device_id_type=pl.DeviceIdType.MESH
        )
    pl.semaphore_wait(barrier, 2 + len(partners))

    def ring_copy(h):
        return pltpu.make_async_remote_copy(
            src_ref=outgoing.at[h], dst_ref=incoming.at[h],
            send_sem=ring_send.at[h], recv_sem=ring_recv.at[h],
            device_id=(after, mine), device_id_type=pl.DeviceIdType.MESH,
        )

    def peer_copy(h, d, other):
        start = pl.multiple_of((mine * heads + h) * dim, dim)
        return pltpu.make_async_remote_copy(
            src_ref=stage.at[h, pl.ds(pl.multiple_of(other * rows, rows), rows), :],
            dst_ref=res_ref.at[:, pl.ds(start, dim)],
            send_sem=peer_send.at[h, d], recv_sem=peer_recv.at[h, d],
            device_id=(me, other), device_id_type=pl.DeviceIdType.MESH,
        )

    @pl.when(me == 0)
    def _():
        incoming[...] = jnp.zeros_like(incoming)

    def step(h, carry):
        @pl.when(me > 0)
        def _():
            ring_copy(h).wait_recv()

        state = split(incoming[h])

        @pl.when(me < ring - 1)
        def _():
            outgoing[h] = state_ref[h] + dot3(split(prod_ref[h]), state)
            ring_copy(h).start()

        span = pl.ds(pl.multiple_of(h * dim, dim), dim)
        core = out_ref[:, span] + dot1(eff_ref[:, span].astype(bf16), state[0])
        gate = gate_ref[:, span].astype(f32)
        normed = core * lax.rsqrt(jnp.mean(core * core, axis=-1, keepdims=True) + norm_eps)
        stage[h] = (normed * gain_ref[...] * silu(gate)).astype(bf16)
        for d, other in enumerate(partners):
            peer_copy(h, d, other).start()
        start = pl.multiple_of((mine * heads + h) * dim, dim)
        res_ref[:, pl.ds(start, dim)] = stage[h, pl.ds(pl.multiple_of(mine * rows, rows), rows), :]
        return carry

    lax.fori_loop(0, heads, step, 0)

    def drain(h, carry):
        @pl.when(me < ring - 1)
        def _():
            ring_copy(h).wait_send()

        for d, other in enumerate(partners):
            peer_copy(h, d, other).wait()
        return carry

    lax.fori_loop(0, heads, drain, 0)


def shifted(value, axis, steps):
    count = lax.axis_size(axis)
    first, last = (max(0, -steps), min(count, count - steps))
    return lax.ppermute(value, axis, [(source, source + steps) for source in range(first, last)])


def body(
    query_in, key_in, value_in, query_taps, key_taps, value_taps,
    log_decay, beta_logit, gate_in, norm_gain,
):
    dim = norm_gain.shape[0]
    length = query_in.shape[0]
    value_heads = log_decay.shape[0]
    key_heads = query_in.shape[1] // dim
    ratio = value_heads // key_heads
    taps = query_taps.shape[0]
    tails = shifted(
        jnp.concatenate([query_in[-PAD:], key_in[-PAD:], value_in[-PAD:]], axis=1), "ctx", 1
    )
    wide = ratio * dim

    def block(rows, width, first=0):
        return pl.BlockSpec((rows, width), lambda i: (0, first + i))

    rates = pl.BlockSpec((1, ratio, length), lambda i: (i, 0, 0))
    mats = pl.BlockSpec((ratio, dim, dim), lambda i: (i, 0, 0))
    mat_shape = jax.ShapeDtypeStruct((value_heads, dim, dim), f32)
    wide_shape = jax.ShapeDtypeStruct((length, value_heads * dim), f32)
    local_out, effect, local_state, product = pl.pallas_call(
        local_kernel,
        grid=(key_heads,),
        in_specs=[
            block(length, dim), block(length, dim), block(length, wide),
            block(PAD, dim), block(PAD, dim, key_heads), block(PAD, wide, 2 * key_heads // ratio),
            block(taps, dim), block(taps, dim), block(taps, wide),
            rates, rates,
        ],
        out_specs=[block(length, wide), block(length, wide), mats, mats],
        out_shape=[wide_shape, wide_shape, mat_shape, mat_shape],
        scratch_shapes=[
            pltpu.VMEM((length + PAD, dim), f32),
            pltpu.VMEM((length + PAD, wide), f32),
        ],
        compiler_params=pltpu.CompilerParams(vmem_limit_bytes=48 * 1024 * 1024),
        name="local",
    )(
        query_in, key_in, value_in, tails, tails, tails, query_taps, key_taps, value_taps,
        log_decay.reshape(key_heads, ratio, length), beta_logit.reshape(key_heads, ratio, length),
    )

    ring, peers = lax.axis_size("ctx"), lax.axis_size("head")
    whole = pl.BlockSpec(memory_space=pltpu.VMEM)
    return pl.pallas_call(
        functools.partial(carry_kernel, ring, peers),
        in_specs=[whole] * 6,
        out_specs=whole,
        out_shape=jax.ShapeDtypeStruct((length // peers, peers * value_heads * dim), bf16),
        scratch_shapes=[
            pltpu.VMEM((value_heads, dim, dim), f32),
            pltpu.VMEM((value_heads, dim, dim), f32),
            pltpu.VMEM((value_heads, length, dim), bf16),
            pltpu.SemaphoreType.DMA((value_heads,)),
            pltpu.SemaphoreType.DMA((value_heads,)),
            pltpu.SemaphoreType.DMA((value_heads, peers - 1)),
            pltpu.SemaphoreType.DMA((value_heads, peers - 1)),
        ],
        compiler_params=pltpu.CompilerParams(
            collective_id=0, has_side_effects=True, vmem_limit_bytes=40 * 1024 * 1024
        ),
        name="carry",
    )(local_out, effect, local_state, product, gate_in, norm_gain.reshape(1, dim))


def solution(mesh):
    in_specs = (
        P("ctx", "head"), P("ctx", "head"), P("ctx", "head"),
        P(None, "head"), P(None, "head"), P(None, "head"),
        P("head", "ctx"), P("head", "ctx"), P("ctx", "head"), P(),
    )
    out_specs = P(("ctx", "head"), None)
    return jax.shard_map(body, mesh=mesh, in_specs=in_specs, out_specs=out_specs, check_vma=False)
```

```python
import functools

import jax
import jax.numpy as jnp
from jax import lax
from jax.experimental import pallas as pl
from jax.experimental.pallas import tpu as pltpu
from jax.sharding import PartitionSpec as P

CHUNK = 128
PAD = 16
norm_eps = 1e-06
bf16 = jnp.bfloat16
f32 = jnp.float32
highest = lax.Precision.HIGHEST


def split(x):
    hi = x.astype(bf16)
    return hi, (x - hi.astype(f32)).astype(bf16)


def dot1(a, b):
    return jnp.dot(a, b, preferred_element_type=f32)


def dot3(a, b):
    (ah, al), (bh, bl) = a, b
    return dot1(jnp.concatenate([ah, al], axis=1), jnp.concatenate([bh, bh], axis=0)) + dot1(ah, bl)


def silu(x):
    return x / (1.0 + jnp.exp(-x))


def conv(buf, tail_ref, in_ref, taps_ref):
    length = in_ref.shape[0]
    count = taps_ref.shape[0]
    buf[0:PAD, :] = tail_ref[...].astype(f32)
    buf[PAD:, :] = in_ref[...].astype(f32)
    total = None
    for j in range(count):
        term = taps_ref[j : j + 1, :] * buf[pl.ds(PAD - count + 1 + j, length), :]
        total = term if total is None else total + term
    return silu(total)


def unit(x):
    return x * lax.rsqrt(jnp.sum(x * x, axis=-1, keepdims=True) + norm_eps)


def local_kernel(
    q_ref, k_ref, v_ref, qt_ref, kt_ref, vt_ref, qw_ref, kw_ref, vw_ref, ld_ref, bl_ref,
    out_ref, eff_ref, state_ref, prod_ref, qbuf, vbuf,
):
    length, dim = q_ref.shape
    ratio = v_ref.shape[1] // dim
    q_all = (unit(conv(qbuf, qt_ref, q_ref, qw_ref)) * dim ** (-0.5)).astype(bf16)
    k_all = unit(conv(qbuf, kt_ref, k_ref, kw_ref)).astype(bf16)
    v_all = conv(vbuf, vt_ref, v_ref, vw_ref).astype(bf16)

    size = CHUNK
    rows = lax.broadcasted_iota(jnp.int32, (size, size), 0)
    cols = lax.broadcasted_iota(jnp.int32, (size, size), 1)
    inside = cols <= rows
    strictly = cols < rows
    eye = jnp.where(cols == rows, 1.0, 0.0).astype(f32)
    upper = jnp.where(rows <= cols, 1.0, 0.0).astype(f32)
    apart = rows ^ cols
    masks = []
    width = 1
    while width < size:
        pick = (apart >= width) & (apart < 2 * width)
        masks.append(jnp.where(pick, 1.0, 0.0).astype(bf16))
        width *= 2

    def rate_rows(ref):
        first = pl.program_id(0) * ratio
        return jnp.concatenate([ref[pl.ds(first + h, 1), :] for h in range(ratio)], axis=0)

    beta_all = 1.0 / (1.0 + jnp.exp(-rate_rows(bl_ref)))
    decay_all = rate_rows(ld_ref)
    items = []
    for c in range(length // size):
        span = slice(c * size, (c + 1) * size)
        kc, qc = k_all[span], q_all[span]
        kf, qf = kc.astype(f32), qc.astype(f32)
        k_turn = kf.T
        nt = (((1,), (1,)), ((), ()))
        gram = lax.dot_general(kc, kc, nt, preferred_element_type=f32)
        qk = lax.dot_general(qc, kc, nt, preferred_element_type=f32)
        cum = lax.dot_general(
            decay_all[:, span], upper, (((1,), (0,)), ((), ())),
            precision=highest, preferred_element_type=f32,
        )
        stacked = jnp.concatenate(
            [cum, beta_all[:, span], jnp.zeros((8 - 2 * ratio, size), f32)], axis=0
        )
        turned = stacked.T
        for h in range(ratio):
            cum_row = cum[h : h + 1]
            cum_col = turned[:, h : h + 1]
            beta_col = turned[:, ratio + h : ratio + h + 1]
            last = cum_row[:, size - 1 :]
            mask = jnp.where(inside, jnp.exp(jnp.where(inside, cum_col - cum_row, 0.0)), 0.0)
            low = split(jnp.where(strictly, beta_col * gram * mask, 0.0))
            grow = jnp.exp(cum_col)
            vf = v_all[span, h * dim : (h + 1) * dim].astype(f32)
            items.append(dict(
                c=c, h=h, low=low,
                x=eye - (low[0] * masks[0]).astype(f32) - (low[1] * masks[0]).astype(f32),
                rhs=split(jnp.concatenate([beta_col * vf, (beta_col * grow) * kf], axis=1)),
                scores=(qk * mask),
                qd=qf * grow,
                kd=k_turn * jnp.exp(last - cum_row),
                keep=jnp.exp(last),
            ))
    for mask in masks[1:]:
        for it in items:
            x = it["x"].astype(bf16)
            part = dot1(x, it["low"][0] * mask)
            it["x"] = it["x"] - dot1(part.astype(bf16), x)
    for it in items:
        x = split(it["x"])
        rest = (eye - it["x"]) - dot3(it["low"], x)
        it["x"] = it["x"] + dot1(x[0], rest.astype(bf16))
    for it in items:
        it["uw"] = dot3(split(it["x"]), it["rhs"])
    states = [None] * ratio
    for it in items:
        c, h = it["c"], it["h"]
        u, w = it["uw"][:, :dim], it["uw"][:, dim:]
        zero = jnp.zeros((size, dim), f32)
        if c == 0:
            new = jnp.concatenate([u, -w], axis=1)
            seen = jnp.concatenate([zero, it["qd"]], axis=1)
            kept = jnp.concatenate([jnp.zeros((dim, dim), f32), it["keep"] * eye], axis=1)
        else:
            both = split(jnp.concatenate([w, it["qd"]], axis=0))
            got = dot3(both, split(states[h]))
            new = jnp.concatenate([u, zero], axis=1) - got[:size]
            seen = got[size:]
            kept = it["keep"] * states[h]
        new = split(new)
        out = seen + dot1(it["scores"].astype(bf16), new[0])
        states[h] = kept + dot3(split(it["kd"]), new)
        span = pl.ds(c * size, size)
        out_ref[span, h * dim : (h + 1) * dim] = out[:, :dim]
        eff_ref[span, h * dim : (h + 1) * dim] = out[:, dim:]
    for h in range(ratio):
        state_ref[h] = states[h][:, :dim]
        prod_ref[h] = states[h][:, dim:]


def carry_kernel(
    ring, peers, out_ref, eff_ref, state_ref, prod_ref, gate_ref, gain_ref, res_ref,
    incoming, outgoing, stage, factor, ring_send, ring_recv, peer_send, peer_recv,
):
    heads, dim, _ = state_ref.shape
    rows = res_ref.shape[0]
    me = lax.axis_index("ctx")
    mine = lax.axis_index("head")
    after, before = lax.rem(me + 1, ring), lax.rem(me + ring - 1, ring)
    partners = [lax.rem(mine + d, peers) for d in range(1, peers)]
    barrier = pltpu.get_barrier_semaphore()
    for other in (after, before):
        pl.semaphore_signal(
            barrier, inc=1, device_id=(other, mine), device_id_type=pl.DeviceIdType.MESH
        )
    for other in partners:
        pl.semaphore_signal(
            barrier, inc=1, device_id=(me, other), device_id_type=pl.DeviceIdType.MESH
        )
    pl.semaphore_wait(barrier, 2 + len(partners))

    def ring_copy(h, source):
        return pltpu.make_async_remote_copy(
            src_ref=source.at[h], dst_ref=incoming.at[h],
            send_sem=ring_send.at[h], recv_sem=ring_recv.at[h],
            device_id=(after, mine), device_id_type=pl.DeviceIdType.MESH,
        )

    def peer_copy(h, d, other):
        start = pl.multiple_of((mine * heads + h) * dim, dim)
        return pltpu.make_async_remote_copy(
            src_ref=stage.at[h, pl.ds(pl.multiple_of(other * rows, rows), rows), :],
            dst_ref=res_ref.at[:, pl.ds(start, dim)],
            send_sem=peer_send.at[h, d], recv_sem=peer_recv.at[h, d],
            device_id=(me, other), device_id_type=pl.DeviceIdType.MESH,
        )

    def head_span(h):
        return pl.ds(pl.multiple_of(h * dim, dim), dim)

    @pl.when(me == 0)
    def _():
        def send(h, carry):
            ring_copy(h, state_ref).start()
            return carry

        lax.fori_loop(0, heads, send, 0)
        incoming[...] = jnp.zeros_like(incoming)

    def gates(h, carry):
        factor[h] = gain_ref[...] * silu(gate_ref[:, head_span(h)].astype(f32))
        return carry

    lax.fori_loop(0, heads, gates, 0)

    def step(h, carry):
        @pl.when(me > 0)
        def _():
            ring_copy(h, outgoing).wait_recv()

        state = split(incoming[h])

        @pl.when((me > 0) & (me < ring - 1))
        def _():
            outgoing[h] = state_ref[h] + dot3(split(prod_ref[h]), state)
            ring_copy(h, outgoing).start()

        span = head_span(h)
        core = out_ref[:, span] + dot1(eff_ref[:, span].astype(bf16), state[0])
        scale = lax.rsqrt(jnp.mean(core * core, axis=-1, keepdims=True) + norm_eps)
        stage[h] = (core * scale * factor[h]).astype(bf16)
        for d, other in enumerate(partners):
            peer_copy(h, d, other).start()
        start = pl.multiple_of((mine * heads + h) * dim, dim)
        res_ref[:, pl.ds(start, dim)] = stage[h, pl.ds(pl.multiple_of(mine * rows, rows), rows), :]
        return carry

    lax.fori_loop(0, heads, step, 0)

    def drain(h, carry):
        @pl.when(me < ring - 1)
        def _():
            ring_copy(h, outgoing).wait_send()

        for d, other in enumerate(partners):
            peer_copy(h, d, other).wait()
        return carry

    lax.fori_loop(0, heads, drain, 0)


def shifted(value, axis, steps):
    count = lax.axis_size(axis)
    first, last = (max(0, -steps), min(count, count - steps))
    return lax.ppermute(value, axis, [(source, source + steps) for source in range(first, last)])


def body(
    query_in, key_in, value_in, query_taps, key_taps, value_taps,
    log_decay, beta_logit, gate_in, norm_gain,
):
    dim = norm_gain.shape[0]
    length = query_in.shape[0]
    value_heads = log_decay.shape[0]
    key_heads = query_in.shape[1] // dim
    ratio = value_heads // key_heads
    taps = query_taps.shape[0]
    tails = shifted(
        jnp.concatenate([query_in[-PAD:], key_in[-PAD:], value_in[-PAD:]], axis=1), "ctx", 1
    )
    wide = ratio * dim

    def block(rows, width, first=0):
        return pl.BlockSpec((rows, width), lambda i: (0, first + i))

    rates = pl.BlockSpec((value_heads, length), lambda i: (0, 0))
    mats = pl.BlockSpec((ratio, dim, dim), lambda i: (i, 0, 0))
    mat_shape = jax.ShapeDtypeStruct((value_heads, dim, dim), f32)
    wide_shape = jax.ShapeDtypeStruct((length, value_heads * dim), f32)
    local_out, effect, local_state, product = pl.pallas_call(
        local_kernel,
        grid=(key_heads,),
        in_specs=[
            block(length, dim), block(length, dim), block(length, wide),
            block(PAD, dim), block(PAD, dim, key_heads), block(PAD, wide, 2 * key_heads // ratio),
            block(taps, dim), block(taps, dim), block(taps, wide),
            rates, rates,
        ],
        out_specs=[block(length, wide), block(length, wide), mats, mats],
        out_shape=[wide_shape, wide_shape, mat_shape, mat_shape],
        scratch_shapes=[
            pltpu.VMEM((length + PAD, dim), f32),
            pltpu.VMEM((length + PAD, wide), f32),
        ],
        compiler_params=pltpu.CompilerParams(vmem_limit_bytes=48 * 1024 * 1024),
        name="local",
    )(
        *[
            pltpu.with_memory_space_constraint(array, pltpu.HBM)
            for array in (query_in, key_in, value_in)
        ],
        tails, tails, tails,
        *[
            pltpu.with_memory_space_constraint(array, pltpu.HBM)
            for array in (
                query_taps, key_taps, value_taps, log_decay, beta_logit,
            )
        ],
    )

    ring, peers = lax.axis_size("ctx"), lax.axis_size("head")
    whole = pl.BlockSpec(memory_space=pltpu.VMEM)
    return pl.pallas_call(
        functools.partial(carry_kernel, ring, peers),
        in_specs=[whole] * 6,
        out_specs=whole,
        out_shape=jax.ShapeDtypeStruct((length // peers, peers * value_heads * dim), bf16),
        scratch_shapes=[
            pltpu.VMEM((value_heads, dim, dim), f32),
            pltpu.VMEM((value_heads, dim, dim), f32),
            pltpu.VMEM((value_heads, length, dim), bf16),
            pltpu.VMEM((value_heads, length, dim), f32),
            pltpu.SemaphoreType.DMA((value_heads,)),
            pltpu.SemaphoreType.DMA((value_heads,)),
            pltpu.SemaphoreType.DMA((value_heads, peers - 1)),
            pltpu.SemaphoreType.DMA((value_heads, peers - 1)),
        ],
        compiler_params=pltpu.CompilerParams(
            collective_id=0, has_side_effects=True, vmem_limit_bytes=40 * 1024 * 1024
        ),
        name="carry",
    )(local_out, effect, local_state, product, gate_in, norm_gain.reshape(1, dim))


def solution(mesh):
    in_specs = (
        P("ctx", "head"), P("ctx", "head"), P("ctx", "head"),
        P(None, "head"), P(None, "head"), P(None, "head"),
        P("head", "ctx"), P("head", "ctx"), P("ctx", "head"), P(),
    )
    out_specs = P(("ctx", "head"), None)
    return jax.shard_map(body, mesh=mesh, in_specs=in_specs, out_specs=out_specs, check_vma=False)
```

```python
import functools

import jax
import jax.numpy as jnp
from jax import lax
from jax.experimental import pallas as pl
from jax.experimental.pallas import tpu as pltpu
from jax.sharding import PartitionSpec as P

CHUNK = 128
PAD = 16
norm_eps = 1e-06
bf16 = jnp.bfloat16
f32 = jnp.float32
highest = lax.Precision.HIGHEST


def split(x):
    hi = x.astype(bf16)
    return hi, (x - hi.astype(f32)).astype(bf16)


def dot1(a, b):
    return jnp.dot(a, b, preferred_element_type=f32)


def dot3(a, b):
    (ah, al), (bh, bl) = a, b
    return dot1(jnp.concatenate([ah, al], axis=1), jnp.concatenate([bh, bh], axis=0)) + dot1(ah, bl)


def silu(x):
    return x / (1.0 + jnp.exp(-x))


def conv(buf, tail_ref, in_ref, taps_ref):
    length = in_ref.shape[0]
    count = taps_ref.shape[0]
    buf[0:PAD, :] = tail_ref[...].astype(f32)
    buf[PAD:, :] = in_ref[...].astype(f32)
    total = None
    for j in range(count):
        term = taps_ref[j : j + 1, :] * buf[pl.ds(PAD - count + 1 + j, length), :]
        total = term if total is None else total + term
    return silu(total)


def unit(x):
    return x * lax.rsqrt(jnp.sum(x * x, axis=-1, keepdims=True) + norm_eps)


def local_kernel(
    dim, q_ref, k_ref, v_ref, qt_ref, kt_ref, vt_ref, qw_ref, kw_ref, vw_ref, ld_ref, bl_ref,
    out_ref, eff_ref, state_ref, prod_ref, qbuf, vbuf,
):
    length = q_ref.shape[0]
    group = q_ref.shape[1] // dim
    ratio = v_ref.shape[1] // q_ref.shape[1]
    q_conv = conv(qbuf, qt_ref, q_ref, qw_ref)
    k_conv = conv(qbuf, kt_ref, k_ref, kw_ref)
    q_heads, k_heads = [], []
    for g in range(group):
        lanes = slice(g * dim, (g + 1) * dim)
        q_heads.append((unit(q_conv[:, lanes]) * dim ** (-0.5)).astype(bf16))
        k_heads.append(unit(k_conv[:, lanes]).astype(bf16))
    v_all = conv(vbuf, vt_ref, v_ref, vw_ref).astype(bf16)

    size = CHUNK
    rows = lax.broadcasted_iota(jnp.int32, (size, size), 0)
    cols = lax.broadcasted_iota(jnp.int32, (size, size), 1)
    inside = cols <= rows
    strictly = cols < rows
    eye = jnp.where(cols == rows, 1.0, 0.0).astype(f32)
    upper = jnp.where(rows <= cols, 1.0, 0.0).astype(f32)
    apart = rows ^ cols
    masks = []
    width = 1
    while width < size:
        pick = (apart >= width) & (apart < 2 * width)
        masks.append(jnp.where(pick, 1.0, 0.0).astype(bf16))
        width *= 2

    def rate_rows(ref):
        first = pl.program_id(0) * (group * ratio)
        return jnp.concatenate([ref[pl.ds(first + h, 1), :] for h in range(group * ratio)], axis=0)

    beta_all = 1.0 / (1.0 + jnp.exp(-rate_rows(bl_ref)))
    decay_all = rate_rows(ld_ref)
    items = []
    heads = group * ratio
    for c in range(length // size):
        span = slice(c * size, (c + 1) * size)
        cum = lax.dot_general(
            decay_all[:, span], upper, (((1,), (0,)), ((), ())),
            precision=highest, preferred_element_type=f32,
        )
        stacked = jnp.concatenate(
            [cum, beta_all[:, span], jnp.zeros((-2 * heads % 8, size), f32)][: 3 if -2 * heads % 8 else 2], axis=0
        )
        turned = stacked.T
        for h in range(heads):
            if h % ratio == 0:
                kc, qc = k_heads[h // ratio][span], q_heads[h // ratio][span]
                kf, qf = kc.astype(f32), qc.astype(f32)
                k_turn = kf.T
                nt = (((1,), (1,)), ((), ()))
                gram = lax.dot_general(kc, kc, nt, preferred_element_type=f32)
                qk = lax.dot_general(qc, kc, nt, preferred_element_type=f32)
            cum_row = cum[h : h + 1]
            cum_col = turned[:, h : h + 1]
            beta_col = turned[:, heads + h : heads + h + 1]
            last = cum_row[:, size - 1 :]
            mask = jnp.where(inside, jnp.exp(jnp.where(inside, cum_col - cum_row, 0.0)), 0.0)
            low = split(jnp.where(strictly, beta_col * gram * mask, 0.0))
            grow = jnp.exp(cum_col)
            vf = v_all[span, h * dim : (h + 1) * dim].astype(f32)
            items.append(dict(
                c=c, h=h, low=low,
                x=eye - (low[0] * masks[0]).astype(f32) - (low[1] * masks[0]).astype(f32),
                rhs=split(jnp.concatenate([beta_col * vf, (beta_col * grow) * kf], axis=1)),
                scores=(qk * mask),
                qd=qf * grow,
                kd=k_turn * jnp.exp(last - cum_row),
                keep=jnp.exp(last),
            ))
    for mask in masks[1:]:
        for it in items:
            x = it["x"].astype(bf16)
            part = dot1(x, it["low"][0] * mask)
            it["x"] = it["x"] - dot1(part.astype(bf16), x)
    for it in items:
        x = split(it["x"])
        rest = (eye - it["x"]) - dot3(it["low"], x)
        it["x"] = it["x"] + dot1(x[0], rest.astype(bf16))
    for it in items:
        it["uw"] = dot3(split(it["x"]), it["rhs"])
    states = [None] * heads
    for it in items:
        c, h = it["c"], it["h"]
        u, w = it["uw"][:, :dim], it["uw"][:, dim:]
        zero = jnp.zeros((size, dim), f32)
        if c == 0:
            new = jnp.concatenate([u, -w], axis=1)
            seen = jnp.concatenate([zero, it["qd"]], axis=1)
            kept = jnp.concatenate([jnp.zeros((dim, dim), f32), it["keep"] * eye], axis=1)
        else:
            both = split(jnp.concatenate([w, it["qd"]], axis=0))
            got = dot3(both, split(states[h]))
            new = jnp.concatenate([u, zero], axis=1) - got[:size]
            seen = got[size:]
            kept = it["keep"] * states[h]
        new = split(new)
        out = seen + dot1(it["scores"].astype(bf16), new[0])
        states[h] = kept + dot3(split(it["kd"]), new)
        span = pl.ds(c * size, size)
        out_ref[span, h * dim : (h + 1) * dim] = out[:, :dim]
        eff_ref[span, h * dim : (h + 1) * dim] = out[:, dim:]
    for h in range(heads):
        state_ref[h] = states[h][:, :dim]
        prod_ref[h] = states[h][:, dim:]


def carry_kernel(
    ring, peers, out_ref, eff_ref, state_ref, prod_ref, gate_ref, gain_ref, res_ref,
    incoming, outgoing, stage, factor, ring_send, ring_recv, peer_send, peer_recv,
):
    heads, dim, _ = state_ref.shape
    rows = res_ref.shape[0]
    me = lax.axis_index("ctx")
    mine = lax.axis_index("head")
    after, before = lax.rem(me + 1, ring), lax.rem(me + ring - 1, ring)
    partners = [lax.rem(mine + d, peers) for d in range(1, peers)]
    barrier = pltpu.get_barrier_semaphore()
    for other in (after, before):
        pl.semaphore_signal(
            barrier, inc=1, device_id=(other, mine), device_id_type=pl.DeviceIdType.MESH
        )
    for other in partners:
        pl.semaphore_signal(
            barrier, inc=1, device_id=(me, other), device_id_type=pl.DeviceIdType.MESH
        )
    pl.semaphore_wait(barrier, 2 + len(partners))

    def ring_copy(h, source):
        return pltpu.make_async_remote_copy(
            src_ref=source.at[h], dst_ref=incoming.at[h],
            send_sem=ring_send.at[h], recv_sem=ring_recv.at[h],
            device_id=(after, mine), device_id_type=pl.DeviceIdType.MESH,
        )

    def peer_copy(h, d, other):
        start = pl.multiple_of((mine * heads + h) * dim, dim)
        return pltpu.make_async_remote_copy(
            src_ref=stage.at[h, pl.ds(pl.multiple_of(other * rows, rows), rows), :],
            dst_ref=res_ref.at[:, pl.ds(start, dim)],
            send_sem=peer_send.at[h, d], recv_sem=peer_recv.at[h, d],
            device_id=(me, other), device_id_type=pl.DeviceIdType.MESH,
        )

    def head_span(h):
        return pl.ds(pl.multiple_of(h * dim, dim), dim)

    @pl.when(me == 0)
    def _():
        def send(h, carry):
            outgoing[h] = state_ref[h].astype(bf16)
            ring_copy(h, outgoing).start()
            return carry

        lax.fori_loop(0, heads, send, 0)
        incoming[...] = jnp.zeros_like(incoming)

    def gates(h, carry):
        factor[h] = gain_ref[...] * silu(gate_ref[:, head_span(h)].astype(f32))
        return carry

    lax.fori_loop(0, heads, gates, 0)

    def step(h, carry):
        @pl.when(me > 0)
        def _():
            ring_copy(h, outgoing).wait_recv()

        state = incoming[h]

        @pl.when((me > 0) & (me < ring - 1))
        def _():
            high, low = split(prod_ref[h])
            both = jnp.concatenate([high, low], axis=1)
            moved = dot1(both, jnp.concatenate([state, state], axis=0))
            outgoing[h] = (state_ref[h] + moved).astype(bf16)
            ring_copy(h, outgoing).start()

        span = head_span(h)
        core = out_ref[:, span] + dot1(eff_ref[:, span].astype(bf16), state)
        scale = lax.rsqrt(jnp.mean(core * core, axis=-1, keepdims=True) + norm_eps)
        stage[h] = (core * scale * factor[h]).astype(bf16)
        for d, other in enumerate(partners):
            peer_copy(h, d, other).start()
        start = pl.multiple_of((mine * heads + h) * dim, dim)
        res_ref[:, pl.ds(start, dim)] = stage[h, pl.ds(pl.multiple_of(mine * rows, rows), rows), :]
        return carry

    lax.fori_loop(0, heads, step, 0)

    def drain(h, carry):
        @pl.when(me < ring - 1)
        def _():
            ring_copy(h, outgoing).wait_send()

        for d, other in enumerate(partners):
            peer_copy(h, d, other).wait()
        return carry

    lax.fori_loop(0, heads, drain, 0)


def shifted(value, axis, steps):
    count = lax.axis_size(axis)
    first, last = (max(0, -steps), min(count, count - steps))
    return lax.ppermute(value, axis, [(source, source + steps) for source in range(first, last)])


def body(
    query_in, key_in, value_in, query_taps, key_taps, value_taps,
    log_decay, beta_logit, gate_in, norm_gain,
):
    dim = norm_gain.shape[0]
    length = query_in.shape[0]
    value_heads = log_decay.shape[0]
    key_heads = query_in.shape[1] // dim
    ratio = value_heads // key_heads
    taps = query_taps.shape[0]
    tails = shifted(
        jnp.concatenate([query_in[-PAD:], key_in[-PAD:], value_in[-PAD:]], axis=1), "ctx", 1
    )
    group = 2 if key_heads % 2 == 0 else 1
    narrow, wide = group * dim, group * ratio * dim

    def block(rows, width, first=0):
        return pl.BlockSpec((rows, width), lambda i: (0, first + i))

    rates = pl.BlockSpec((value_heads, length), lambda i: (0, 0))
    mats = pl.BlockSpec((group * ratio, dim, dim), lambda i: (i, 0, 0))
    mat_shape = jax.ShapeDtypeStruct((value_heads, dim, dim), f32)
    wide_shape = jax.ShapeDtypeStruct((length, value_heads * dim), f32)
    local_out, effect, local_state, product = pl.pallas_call(
        functools.partial(local_kernel, dim),
        grid=(key_heads // group,),
        in_specs=[
            block(length, narrow), block(length, narrow), block(length, wide),
            block(PAD, narrow), block(PAD, narrow, key_heads // group),
            block(PAD, wide, 2 * key_heads // (ratio * group)),
            block(taps, narrow), block(taps, narrow), block(taps, wide),
            rates, rates,
        ],
        out_specs=[block(length, wide), block(length, wide), mats, mats],
        out_shape=[wide_shape, wide_shape, mat_shape, mat_shape],
        scratch_shapes=[
            pltpu.VMEM((length + PAD, narrow), f32),
            pltpu.VMEM((length + PAD, wide), f32),
        ],
        compiler_params=pltpu.CompilerParams(vmem_limit_bytes=48 * 1024 * 1024),
        name="local",
    )(
        *[
            pltpu.with_memory_space_constraint(array, pltpu.HBM)
            for array in (query_in, key_in, value_in)
        ],
        tails, tails, tails,
        *[
            pltpu.with_memory_space_constraint(array, pltpu.HBM)
            for array in (
                query_taps, key_taps, value_taps, log_decay, beta_logit,
            )
        ],
    )

    ring, peers = lax.axis_size("ctx"), lax.axis_size("head")
    whole = pl.BlockSpec(memory_space=pltpu.VMEM)
    return pl.pallas_call(
        functools.partial(carry_kernel, ring, peers),
        in_specs=[whole] * 6,
        out_specs=whole,
        out_shape=jax.ShapeDtypeStruct((length // peers, peers * value_heads * dim), bf16),
        scratch_shapes=[
            pltpu.VMEM((value_heads, dim, dim), bf16),
            pltpu.VMEM((value_heads, dim, dim), bf16),
            pltpu.VMEM((value_heads, length, dim), bf16),
            pltpu.VMEM((value_heads, length, dim), f32),
            pltpu.SemaphoreType.DMA((value_heads,)),
            pltpu.SemaphoreType.DMA((value_heads,)),
            pltpu.SemaphoreType.DMA((value_heads, peers - 1)),
            pltpu.SemaphoreType.DMA((value_heads, peers - 1)),
        ],
        compiler_params=pltpu.CompilerParams(
            collective_id=0, has_side_effects=True, vmem_limit_bytes=40 * 1024 * 1024
        ),
        name="carry",
    )(local_out, effect, local_state, product, gate_in, norm_gain.reshape(1, dim))


def solution(mesh):
    in_specs = (
        P("ctx", "head"), P("ctx", "head"), P("ctx", "head"),
        P(None, "head"), P(None, "head"), P(None, "head"),
        P("head", "ctx"), P("head", "ctx"), P("ctx", "head"), P(),
    )
    out_specs = P(("ctx", "head"), None)
    return jax.shard_map(body, mesh=mesh, in_specs=in_specs, out_specs=out_specs, check_vma=False)
```

```python
import functools

import jax
import jax.numpy as jnp
from jax import lax
from jax.experimental import pallas as pl
from jax.experimental.pallas import tpu as pltpu
from jax.sharding import PartitionSpec as P

CHUNK = 128
PAD = 16
norm_eps = 1e-06
bf16 = jnp.bfloat16
f32 = jnp.float32
highest = lax.Precision.HIGHEST


def split(x):
    hi = x.astype(bf16)
    return hi, (x - hi.astype(f32)).astype(bf16)


def dot1(a, b):
    return jnp.dot(a, b, preferred_element_type=f32)


def dot3(a, b):
    (ah, al), (bh, bl) = a, b
    return dot1(jnp.concatenate([ah, al], axis=1), jnp.concatenate([bh, bh], axis=0)) + dot1(ah, bl)


def silu(x):
    return x / (1.0 + jnp.exp(-x))


def conv(buf, tail_ref, in_ref, taps_ref):
    length = in_ref.shape[0]
    count = taps_ref.shape[0]
    buf[0:PAD, :] = tail_ref[...].astype(f32)
    buf[PAD:, :] = in_ref[...].astype(f32)
    total = None
    for j in range(count):
        term = taps_ref[j : j + 1, :] * buf[pl.ds(PAD - count + 1 + j, length), :]
        total = term if total is None else total + term
    return silu(total)


def unit(x):
    return x * lax.rsqrt(jnp.sum(x * x, axis=-1, keepdims=True) + norm_eps)


def local_kernel(
    dim, q_ref, k_ref, v_ref, qt_ref, kt_ref, vt_ref, qw_ref, kw_ref, vw_ref, ld_ref, bl_ref,
    out_ref, eff_ref, state_ref, prod_ref, qbuf, vbuf,
):
    length = q_ref.shape[0]
    group = q_ref.shape[1] // dim
    ratio = v_ref.shape[1] // q_ref.shape[1]
    q_conv = conv(qbuf, qt_ref, q_ref, qw_ref)
    k_conv = conv(qbuf, kt_ref, k_ref, kw_ref)
    q_heads, k_heads = [], []
    for g in range(group):
        lanes = slice(g * dim, (g + 1) * dim)
        q_heads.append((unit(q_conv[:, lanes]) * dim ** (-0.5)).astype(bf16))
        k_heads.append(unit(k_conv[:, lanes]).astype(bf16))
    v_all = conv(vbuf, vt_ref, v_ref, vw_ref).astype(bf16)

    size = CHUNK
    rows = lax.broadcasted_iota(jnp.int32, (size, size), 0)
    cols = lax.broadcasted_iota(jnp.int32, (size, size), 1)
    inside = cols <= rows
    strictly = cols < rows
    eye = jnp.where(cols == rows, 1.0, 0.0).astype(f32)
    upper = jnp.where(rows <= cols, 1.0, 0.0).astype(f32)
    apart = rows ^ cols
    masks = []
    width = 1
    while width < size:
        pick = (apart >= width) & (apart < 2 * width)
        masks.append(jnp.where(pick, 1.0, 0.0).astype(bf16))
        width *= 2

    def rate_rows(ref):
        first = pl.program_id(0) * (group * ratio)
        return jnp.concatenate([ref[pl.ds(first + h, 1), :] for h in range(group * ratio)], axis=0)

    beta_all = 1.0 / (1.0 + jnp.exp(-rate_rows(bl_ref)))
    decay_all = rate_rows(ld_ref)
    items = []
    heads = group * ratio
    for c in range(length // size):
        span = slice(c * size, (c + 1) * size)
        cum = lax.dot_general(
            decay_all[:, span], upper, (((1,), (0,)), ((), ())),
            precision=highest, preferred_element_type=f32,
        )
        stacked = jnp.concatenate(
            [cum, beta_all[:, span], jnp.zeros((-2 * heads % 8, size), f32)][: 3 if -2 * heads % 8 else 2], axis=0
        )
        turned = stacked.T
        for h in range(heads):
            if h % ratio == 0:
                kc, qc = k_heads[h // ratio][span], q_heads[h // ratio][span]
                kf, qf = kc.astype(f32), qc.astype(f32)
                k_turn = kf.T
                nt = (((1,), (1,)), ((), ()))
                gram = lax.dot_general(kc, kc, nt, preferred_element_type=f32)
                qk = lax.dot_general(qc, kc, nt, preferred_element_type=f32)
            cum_row = cum[h : h + 1]
            cum_col = turned[:, h : h + 1]
            beta_col = turned[:, heads + h : heads + h + 1]
            last = cum_row[:, size - 1 :]
            mask = jnp.where(inside, jnp.exp(jnp.where(inside, cum_col - cum_row, 0.0)), 0.0)
            low = split(jnp.where(strictly, beta_col * gram * mask, 0.0))
            grow = jnp.exp(cum_col)
            vf = v_all[span, h * dim : (h + 1) * dim].astype(f32)
            items.append(dict(
                c=c, h=h, low=low,
                x=eye - (low[0] * masks[0]).astype(f32) - (low[1] * masks[0]).astype(f32),
                rhs=split(jnp.concatenate([beta_col * vf, (beta_col * grow) * kf], axis=1)),
                scores=(qk * mask),
                qd=qf * grow,
                kd=k_turn * jnp.exp(last - cum_row),
                keep=jnp.exp(last),
            ))
    for mask in masks[1:]:
        for it in items:
            x = it["x"].astype(bf16)
            part = dot1(x, it["low"][0] * mask)
            it["x"] = it["x"] - dot1(part.astype(bf16), x)
    for it in items:
        x = split(it["x"])
        rest = (eye - it["x"]) - dot3(it["low"], x)
        it["x"] = it["x"] + dot1(x[0], rest.astype(bf16))
    for it in items:
        it["uw"] = dot3(split(it["x"]), it["rhs"])
    states = [None] * heads
    for it in items:
        c, h = it["c"], it["h"]
        u, w = it["uw"][:, :dim], it["uw"][:, dim:]
        zero = jnp.zeros((size, dim), f32)
        if c == 0:
            new = jnp.concatenate([u, -w], axis=1)
            seen = jnp.concatenate([zero, it["qd"]], axis=1)
            kept = jnp.concatenate([jnp.zeros((dim, dim), f32), it["keep"] * eye], axis=1)
        else:
            both = jnp.concatenate([w, it["qd"]], axis=0).astype(bf16)
            got = dot1(both, states[h].astype(bf16))
            new = jnp.concatenate([u, zero], axis=1) - got[:size]
            seen = got[size:]
            kept = it["keep"] * states[h]
        new = split(new)
        out = seen + dot1(it["scores"].astype(bf16), new[0])
        states[h] = kept + dot3(split(it["kd"]), new)
        span = pl.ds(c * size, size)
        out_ref[span, h * dim : (h + 1) * dim] = out[:, :dim]
        eff_ref[span, h * dim : (h + 1) * dim] = out[:, dim:]
    for h in range(heads):
        state_ref[h] = states[h][:, :dim]
        prod_ref[h] = states[h][:, dim:]


def carry_kernel(
    ring, peers, out_ref, eff_ref, state_ref, prod_ref, gate_ref, gain_ref, res_ref,
    incoming, outgoing, stage, factor, ring_send, ring_recv, peer_send, peer_recv,
):
    heads, dim, _ = state_ref.shape
    rows = res_ref.shape[0]
    me = lax.axis_index("ctx")
    mine = lax.axis_index("head")
    after, before = lax.rem(me + 1, ring), lax.rem(me + ring - 1, ring)
    partners = [lax.rem(mine + d, peers) for d in range(1, peers)]
    barrier = pltpu.get_barrier_semaphore()
    for other in (after, before):
        pl.semaphore_signal(
            barrier, inc=1, device_id=(other, mine), device_id_type=pl.DeviceIdType.MESH
        )
    for other in partners:
        pl.semaphore_signal(
            barrier, inc=1, device_id=(me, other), device_id_type=pl.DeviceIdType.MESH
        )
    pl.semaphore_wait(barrier, 2 + len(partners))

    def ring_copy(h, source):
        return pltpu.make_async_remote_copy(
            src_ref=source.at[h], dst_ref=incoming.at[h],
            send_sem=ring_send.at[h], recv_sem=ring_recv.at[h],
            device_id=(after, mine), device_id_type=pl.DeviceIdType.MESH,
        )

    def peer_copy(h, d, other):
        start = pl.multiple_of((mine * heads + h) * dim, dim)
        return pltpu.make_async_remote_copy(
            src_ref=stage.at[h, pl.ds(pl.multiple_of(other * rows, rows), rows), :],
            dst_ref=res_ref.at[:, pl.ds(start, dim)],
            send_sem=peer_send.at[h, d], recv_sem=peer_recv.at[h, d],
            device_id=(me, other), device_id_type=pl.DeviceIdType.MESH,
        )

    def head_span(h):
        return pl.ds(pl.multiple_of(h * dim, dim), dim)

    @pl.when(me == 0)
    def _():
        def send(h, carry):
            outgoing[h] = state_ref[h].astype(bf16)
            ring_copy(h, outgoing).start()
            return carry

        lax.fori_loop(0, heads, send, 0)
        incoming[...] = jnp.zeros_like(incoming)

    def gates(h, carry):
        factor[h] = gain_ref[...] * silu(gate_ref[:, head_span(h)].astype(f32))
        return carry

    lax.fori_loop(0, heads, gates, 0)

    def step(h, carry):
        @pl.when(me > 0)
        def _():
            ring_copy(h, outgoing).wait_recv()

        state = incoming[h]

        @pl.when((me > 0) & (me < ring - 1))
        def _():
            high, low = split(prod_ref[h])
            both = jnp.concatenate([high, low], axis=1)
            moved = dot1(both, jnp.concatenate([state, state], axis=0))
            outgoing[h] = (state_ref[h] + moved).astype(bf16)
            ring_copy(h, outgoing).start()

        span = head_span(h)
        core = out_ref[:, span] + dot1(eff_ref[:, span].astype(bf16), state)
        scale = lax.rsqrt(jnp.mean(core * core, axis=-1, keepdims=True) + norm_eps)
        stage[h] = (core * scale * factor[h]).astype(bf16)
        for d, other in enumerate(partners):
            peer_copy(h, d, other).start()
        start = pl.multiple_of((mine * heads + h) * dim, dim)
        res_ref[:, pl.ds(start, dim)] = stage[h, pl.ds(pl.multiple_of(mine * rows, rows), rows), :]
        return carry

    lax.fori_loop(0, heads, step, 0)

    def drain(h, carry):
        @pl.when(me < ring - 1)
        def _():
            ring_copy(h, outgoing).wait_send()

        for d, other in enumerate(partners):
            peer_copy(h, d, other).wait()
        return carry

    lax.fori_loop(0, heads, drain, 0)


def shifted(value, axis, steps):
    count = lax.axis_size(axis)
    first, last = (max(0, -steps), min(count, count - steps))
    return lax.ppermute(value, axis, [(source, source + steps) for source in range(first, last)])


def body(
    query_in, key_in, value_in, query_taps, key_taps, value_taps,
    log_decay, beta_logit, gate_in, norm_gain,
):
    dim = norm_gain.shape[0]
    length = query_in.shape[0]
    value_heads = log_decay.shape[0]
    key_heads = query_in.shape[1] // dim
    ratio = value_heads // key_heads
    taps = query_taps.shape[0]
    tails = shifted(
        jnp.concatenate([query_in[-PAD:], key_in[-PAD:], value_in[-PAD:]], axis=1), "ctx", 1
    )
    group = 2 if key_heads % 2 == 0 else 1
    narrow, wide = group * dim, group * ratio * dim

    def block(rows, width, first=0):
        return pl.BlockSpec((rows, width), lambda i: (0, first + i))

    rates = pl.BlockSpec((value_heads, length), lambda i: (0, 0))
    mats = pl.BlockSpec((group * ratio, dim, dim), lambda i: (i, 0, 0))
    mat_shape = jax.ShapeDtypeStruct((value_heads, dim, dim), f32)
    wide_shape = jax.ShapeDtypeStruct((length, value_heads * dim), f32)
    local_out, effect, local_state, product = pl.pallas_call(
        functools.partial(local_kernel, dim),
        grid=(key_heads // group,),
        in_specs=[
            block(length, narrow), block(length, narrow), block(length, wide),
            block(PAD, narrow), block(PAD, narrow, key_heads // group),
            block(PAD, wide, 2 * key_heads // (ratio * group)),
            block(taps, narrow), block(taps, narrow), block(taps, wide),
            rates, rates,
        ],
        out_specs=[block(length, wide), block(length, wide), mats, mats],
        out_shape=[wide_shape, wide_shape, mat_shape, mat_shape],
        scratch_shapes=[
            pltpu.VMEM((length + PAD, narrow), f32),
            pltpu.VMEM((length + PAD, wide), f32),
        ],
        compiler_params=pltpu.CompilerParams(vmem_limit_bytes=48 * 1024 * 1024),
        name="local",
    )(
        *[
            pltpu.with_memory_space_constraint(array, pltpu.HBM)
            for array in (query_in, key_in, value_in)
        ],
        tails, tails, tails,
        *[
            pltpu.with_memory_space_constraint(array, pltpu.HBM)
            for array in (
                query_taps, key_taps, value_taps, log_decay, beta_logit,
            )
        ],
    )

    ring, peers = lax.axis_size("ctx"), lax.axis_size("head")
    whole = pl.BlockSpec(memory_space=pltpu.VMEM)
    return pl.pallas_call(
        functools.partial(carry_kernel, ring, peers),
        in_specs=[whole] * 6,
        out_specs=whole,
        out_shape=jax.ShapeDtypeStruct((length // peers, peers * value_heads * dim), bf16),
        scratch_shapes=[
            pltpu.VMEM((value_heads, dim, dim), bf16),
            pltpu.VMEM((value_heads, dim, dim), bf16),
            pltpu.VMEM((value_heads, length, dim), bf16),
            pltpu.VMEM((value_heads, length, dim), f32),
            pltpu.SemaphoreType.DMA((value_heads,)),
            pltpu.SemaphoreType.DMA((value_heads,)),
            pltpu.SemaphoreType.DMA((value_heads, peers - 1)),
            pltpu.SemaphoreType.DMA((value_heads, peers - 1)),
        ],
        compiler_params=pltpu.CompilerParams(
            collective_id=0, has_side_effects=True, vmem_limit_bytes=40 * 1024 * 1024
        ),
        name="carry",
    )(local_out, effect, local_state, product, gate_in, norm_gain.reshape(1, dim))


def solution(mesh):
    in_specs = (
        P("ctx", "head"), P("ctx", "head"), P("ctx", "head"),
        P(None, "head"), P(None, "head"), P(None, "head"),
        P("head", "ctx"), P("head", "ctx"), P("ctx", "head"), P(),
    )
    out_specs = P(("ctx", "head"), None)
    return jax.shard_map(body, mesh=mesh, in_specs=in_specs, out_specs=out_specs, check_vma=False)
```
